32 devices in a mesh: shard: 16 (over z, y, core), tensor: 2 (over x).
Axes of the slice: x: 2, y: 2, z: 4, core: 2. Of those that a mesh axis runs over, the one named last changes fastest.
Arguments:
- grads: float32 [16, 2048, 1024], P(None, 'shard', 'tensor'), may hold values from -16 to 16
- momentum: bfloat16 [16, 2048, 1024], P(None, 'shard', 'tensor'), may hold values from -32 to 32
- counts: int32 [1], replicated, may hold values from 1 to 8
- emb_grad: float32 [8192, 2048], P('shard', 'tensor'), may hold values from -6 to 6
- emb_weight: float32 [8192, 2048], P('shard', 'tensor'), may hold values from -6 to 6
- emb_first: float32 [8192, 2048], P('shard', 'tensor'), may hold values from -2 to 2
- emb_second: float32 [8192, 2048], P('shard', 'tensor'), may hold values from 0.01 to 1
- gain_grad: float32 [16384], P(('shard', 'tensor')), may hold values from -6 to 6
- gain_weight: float32 [16384], P(('shard', 'tensor')), may hold values from 0.5 to 1.5
- gain_first: float32 [16384], P(('shard', 'tensor')), may hold values from -2 to 2
- gain_second: float32 [16384], P(('shard', 'tensor')), may hold values from 0.01 to 1
Outputs:
- new_momentum: bfloat16 [16, 2048, 1024], P(None, 'shard', 'tensor')
- update: float32 [16, 2048, 1024], P(None, 'shard', 'tensor')
- emb_weight_new: float32 [8192, 2048], P('shard', 'tensor')
- emb_first_new: float32 [8192, 2048], P('shard', 'tensor')
- emb_second_new: float32 [8192, 2048], P('shard', 'tensor')
- gain_weight_new: float32 [16384], P(('shard', 'tensor'))
- gain_first_new: float32 [16384], P(('shard', 'tensor'))
- gain_second_new: float32 [16384], P(('shard', 'tensor'))
The draws below stay inside these ranges and needn't reach their ends.
All inputs are finite; a program needn't handle non-finite values.
Results may differ from the reference program's by a relative error of at most 0.012.
The reference program's roundings to bfloat16 on the way count: a program that leaves them out, or rounds other values in their place, can miss the bound.
Values may be sent and summed in bfloat16 or wider, within the bound.
No kernel may reach another device: no remote copies, remote signals or barrier semaphores. Data moves between devices by JAX's collectives and lax.ppermute only.
A program may use at most 128 MiB of HBM per device.

```python
import math
import jax
import jax.numpy as jnp
from jax import lax

D = 2048
INNER = 1024
NS_STEPS = 4
NMAT = 16
VROWS = 8192
GAINS = 16384


rank_weights = (1.0, 0.7, 0.5, 0.35)


def column_field(key, factor):
    position = jnp.arange(INNER, dtype=jnp.float32) / max(INNER - 1, 1)
    profile = jnp.exp(position * jnp.log(factor))
    values = 0.6 * jnp.clip(jax.random.normal(key, (NMAT, D, INNER), jnp.float32), -3.0, 3.0)
    return values * profile[None, None, :]


def common_part(key, amplitude):
    anchor = jax.random.fold_in(key, 5)
    left_factor = jnp.clip(jax.random.normal(jax.random.fold_in(anchor, 1), (NMAT, D, 4), jnp.float32), -2.5, 2.5)
    right_factor = jnp.clip(jax.random.normal(jax.random.fold_in(anchor, 2), (NMAT, 4, INNER), jnp.float32), -2.5, 2.5)
    summed = jnp.zeros((NMAT, D, INNER), jnp.float32)
    for number in range(4):
        weight_now = amplitude * rank_weights[number]
        summed = summed + weight_now * left_factor[:, :, number][:, :, None] * right_factor[:, number, :][:, None, :]
    return summed


def shared_field(key, salt):
    bulk = column_field(jax.random.fold_in(key, salt), 4.0)
    amplitude = 1.9
    return jnp.clip(bulk + common_part(key, amplitude), -15.5, 15.5)


def draw_grads(key, part):
    return shared_field(key, 11)


def draw_momentum(key, part):
    return (2.0 * shared_field(key, 23)).astype(jnp.bfloat16)


def shard_levels(own_key, shape, cuts, smallest, high):
    loudness, own = 1.0, jax.random.fold_in(own_key, 6)
    for dim, blocks in cuts:
        steps = jnp.exp(jax.random.uniform(jax.random.fold_in(own, dim), (blocks,), jnp.float32, smallest / len(cuts), high / len(cuts)))
        loudness = loudness * jnp.repeat(steps, shape[dim] // blocks).reshape([-1 if axis == dim else 1 for axis in range(len(shape))])
    return loudness


def gaussian(own_key, shape, deviation, most, pieces=(), held_as=jnp.bfloat16):
    loudness = shard_levels(own_key, shape, pieces, -0.22, 0.18) if pieces else 1.0
    drawn = jax.random.normal(own_key, shape, jnp.float32) * deviation * loudness
    return jnp.minimum(jnp.maximum(drawn, -most), most).astype(held_as)


def setup_inputs(seed: int = 0) -> dict:
    arg_keys = jax.random.split(jax.random.key(seed), 12)
    grads = draw_grads(jax.random.fold_in(arg_keys[11], 71), 0)
    momentum = draw_momentum(jax.random.fold_in(arg_keys[11], 71), 0)
    counts = jax.random.randint(arg_keys[2], (1,), 1, 9).astype(jnp.int32)
    emb_grad = gaussian(arg_keys[3], (VROWS, D), 1.0, 6.0, ((0, 16), (1, 2)), jnp.float32)
    emb_weight = gaussian(arg_keys[4], (VROWS, D), 1.0, 6.0, ((0, 16), (1, 2)), jnp.float32)
    emb_first = gaussian(arg_keys[5], (VROWS, D), 0.3, 2.0, ((0, 16), (1, 2)), jnp.float32)
    emb_second = jnp.clip(jnp.exp(math.log(1.0) - 4.6051702 * jax.random.uniform(arg_keys[6], (VROWS, D), jnp.float32) ** shard_levels(arg_keys[6], (VROWS, D), ((0, 16), (1, 2)), -0.2, 0.2)), 0.01, 1.0)
    gain_grad = gaussian(arg_keys[7], (GAINS,), 1.0, 6.0, ((0, 32),), jnp.float32)
    gain_weight = jnp.clip(1.0 + 0.1 * jax.random.normal(arg_keys[8], (GAINS,), jnp.float32), 0.5, 1.5)
    gain_first = gaussian(arg_keys[9], (GAINS,), 0.3, 2.0, ((0, 32),), jnp.float32)
    gain_second = jnp.clip(jnp.exp(math.log(1.0) - 4.6051702 * jax.random.uniform(arg_keys[10], (GAINS,), jnp.float32) ** shard_levels(arg_keys[10], (GAINS,), ((0, 32),), -0.2, 0.2)), 0.01, 1.0)
    return {"grads": grads, "momentum": momentum, "counts": counts, "emb_grad": emb_grad, "emb_weight": emb_weight, "emb_first": emb_first, "emb_second": emb_second, "gain_grad": gain_grad, "gain_weight": gain_weight, "gain_first": gain_first, "gain_second": gain_second}


linear_coef = 3.4445
cubic_coef = -4.775
quintic_coef = 2.0315
momentum_rate = 0.95
learn_rate = 0.01
decay_weight = 0.1
first_rate = 0.9
second_rate = 0.95
adam_floor = 1e-08
norm_floor = 1e-07

def adamw(grad, weight, first, second, inverse):
    scaled = grad * inverse
    first_new = first_rate * first + (1.0 - first_rate) * scaled
    second_new = second_rate * second + (1.0 - second_rate) * scaled * scaled
    weight_new = weight - learn_rate * (first_new / (jnp.sqrt(second_new) + adam_floor) + decay_weight * weight)
    return (weight_new, first_new, second_new)

def orthogonalize(matrix):
    total = jnp.sqrt(jnp.sum(matrix * matrix))
    iterate = (matrix / (total + norm_floor)).astype(jnp.bfloat16)
    result = jnp.zeros(matrix.shape, jnp.float32)
    for number in range(NS_STEPS):
        gram = jnp.dot(iterate.T, iterate, preferred_element_type=jnp.float32).astype(jnp.bfloat16)
        product = jnp.dot(iterate, gram, preferred_element_type=jnp.float32)
        quintic = jnp.dot(product.astype(jnp.bfloat16), gram, preferred_element_type=jnp.float32)
        mixed = linear_coef * iterate.astype(jnp.float32) + cubic_coef * product + quintic_coef * quintic
        if number + 1 == NS_STEPS:
            result = mixed * math.sqrt(D)
        else:
            iterate = mixed.astype(jnp.bfloat16)
    return result

def reference(grads, momentum, counts, emb_grad, emb_weight, emb_first, emb_second, gain_grad, gain_weight, gain_first, gain_second):
    inverse = 1.0 / counts[0].astype(jnp.float32)
    scaled = grads * inverse
    velocity = momentum_rate * momentum.astype(jnp.float32) + scaled
    advance = scaled + momentum_rate * velocity
    update = lax.map(orthogonalize, advance)
    emb_new = adamw(emb_grad, emb_weight, emb_first, emb_second, inverse)
    gain_new = adamw(gain_grad, gain_weight, gain_first, gain_second, inverse)
    return (velocity.astype(jnp.bfloat16), update, emb_new[0], emb_new[1], emb_new[2], gain_new[0], gain_new[1], gain_new[2])
```

```python
import functools
import math

import jax
import jax.numpy as jnp
from jax import lax
from jax.experimental import pallas as pl
from jax.experimental.pallas import tpu as pltpu
from jax.sharding import PartitionSpec as P

D = 2048
NS_STEPS = 4
CORES = 2
EDGE = 256
LIFT = 512.0

linear_coef = 3.4445
cubic_coef = -4.775
quintic_coef = 2.0315
momentum_rate = 0.95
learn_rate = 0.01
decay_weight = 0.1
first_rate = 0.9
second_rate = 0.95
adam_floor = 1e-08
norm_floor = 1e-07


def adamw(grad, weight, first, second, inverse):
    scaled = grad * inverse
    first_new = first_rate * first + (1.0 - first_rate) * scaled
    second_new = second_rate * second + (1.0 - second_rate) * scaled * scaled
    weight_new = weight - learn_rate * (
        first_new / (jnp.sqrt(second_new) + adam_floor) + decay_weight * weight
    )
    return (weight_new, first_new, second_new)


def span(index):
    return slice(index * EDGE, (index + 1) * EDGE)


def upper_blocks(width):
    return [(i, j) for j in range(width // EDGE) for i in range(j + 1)]


def write_gram(turned_ref, gram_ref):
    slot = 0
    for j in range(turned_ref.shape[0] // EDGE):
        part = lax.dot_general(
            turned_ref[: (j + 1) * EDGE, :],
            turned_ref[span(j), :],
            (((1,), (1,)), ((), ())),
            preferred_element_type=jnp.float32,
        )
        for i in range(j + 1):
            gram_ref[slot] = part[span(i), :].astype(jnp.bfloat16)
            slot += 1


def write_poly(own_ref, other_ref, gram, poly):
    for slot, (i, j) in enumerate(upper_blocks(gram.shape[0])):
        block = own_ref[slot].astype(jnp.float32) + other_ref[slot].astype(jnp.float32)
        block = block.astype(jnp.bfloat16)
        gram[span(i), span(j)] = block
        if i != j:
            gram[span(j), span(i)] = block.T
    for j in range(gram.shape[0] // EDGE):
        square = jnp.dot(
            gram[: (j + 1) * EDGE, :], gram[:, span(j)], preferred_element_type=jnp.float32
        )
        for i in range(j + 1):
            block = cubic_coef * gram[span(i), span(j)].astype(jnp.float32)
            block = (block + quintic_coef * square[span(i), :]).astype(jnp.bfloat16)
            poly[span(i), span(j)] = block
            if i != j:
                poly[span(j), span(i)] = block.T


def first_kernel(block_ref, turned_ref, gram_ref, *, tensor):
    blocks, rows, cols = block_ref.shape
    for s in range(blocks // tensor):
        for t in range(tensor):
            turned_ref[t * cols : (t + 1) * cols, s * rows : (s + 1) * rows] = block_ref[
                s * tensor + t
            ].T
    write_gram(turned_ref, gram_ref)


def middle_kernel(turned_ref, own_ref, other_ref, next_ref, gram_ref, gram, poly):
    write_poly(own_ref, other_ref, gram, poly)
    for c in range(turned_ref.shape[1] // EDGE):
        old = turned_ref[:, span(c)]
        new = linear_coef * old.astype(jnp.float32) + jnp.dot(
            poly[...], old, preferred_element_type=jnp.float32
        )
        next_ref[:, span(c)] = new.astype(jnp.bfloat16)
    write_gram(next_ref, gram_ref)


def last_kernel(turned_ref, own_ref, other_ref, block_ref, gram, poly, *, tensor):
    write_poly(own_ref, other_ref, gram, poly)
    blocks, rows, cols = block_ref.shape
    for s in range(blocks // tensor):
        old = turned_ref[:, s * rows : (s + 1) * rows].T
        new = linear_coef * old.astype(jnp.float32) + jnp.dot(
            old, poly[...], preferred_element_type=jnp.float32
        )
        new = (math.sqrt(D) * new).astype(jnp.bfloat16)
        for t in range(tensor):
            block_ref[s * tensor + t] = new[:, t * cols : (t + 1) * cols]


def run_kernel(kernel, results, scratch, *operands):
    whole = pl.BlockSpec(memory_space=pltpu.VMEM)
    return pl.pallas_call(
        kernel,
        out_shape=results,
        in_specs=[whole] * len(operands),
        out_specs=[whole] * len(results),
        scratch_shapes=scratch,
        compiler_params=pltpu.CompilerParams(vmem_limit_bytes=48 * 2**20),
    )(*operands)


def other_core(value):
    shards = lax.axis_size("shard")
    return lax.ppermute(value, "shard", [(i, i ^ 1) for i in range(shards)])


def chip_groups():
    shards, tensor = lax.axis_size("shard"), lax.axis_size("tensor")
    return [
        [s * tensor + t for s in range(core, shards, CORES) for t in range(tensor)]
        for core in range(CORES)
    ]


def exchange(blocks):
    return lax.all_to_all(
        blocks,
        ("shard", "tensor"),
        split_axis=0,
        concat_axis=0,
        axis_index_groups=chip_groups(),
        tiled=True,
    )


def orthogonalize(blocks):
    tensor = lax.axis_size("tensor")
    width = tensor * blocks.shape[2]
    height = blocks.shape[0] // tensor * blocks.shape[1]
    turned_type = jax.ShapeDtypeStruct((width, height), jnp.bfloat16)
    gram_type = jax.ShapeDtypeStruct((len(upper_blocks(width)), EDGE, EDGE), jnp.bfloat16)
    squares = [pltpu.VMEM((width, width), jnp.bfloat16)] * 2
    turned, own = run_kernel(
        functools.partial(first_kernel, tensor=tensor), [turned_type, gram_type], [], blocks
    )
    for _ in range(NS_STEPS - 1):
        turned, own = run_kernel(
            middle_kernel, [turned_type, gram_type], squares, turned, own, other_core(own)
        )
    return run_kernel(
        functools.partial(last_kernel, tensor=tensor),
        [jax.ShapeDtypeStruct(blocks.shape, jnp.bfloat16)],
        squares,
        turned,
        own,
        other_core(own),
    )[0]


def body(
    grads,
    momentum,
    counts,
    emb_grad,
    emb_weight,
    emb_first,
    emb_second,
    gain_grad,
    gain_weight,
    gain_first,
    gain_second,
):
    inverse = 1.0 / counts[0].astype(jnp.float32)
    scaled = grads * inverse
    velocity = momentum_rate * momentum.astype(jnp.float32) + scaled
    advance = scaled + momentum_rate * velocity
    owned = exchange((advance * LIFT).astype(jnp.float16)).astype(jnp.float32) / LIFT
    total = jnp.sum(owned * owned)
    total = jnp.sqrt(total + other_core(total))
    iterate = (owned / (total + norm_floor)).astype(jnp.bfloat16)
    update = exchange(orthogonalize(iterate)).astype(jnp.float32)
    emb_new = adamw(emb_grad, emb_weight, emb_first, emb_second, inverse)
    gain_new = adamw(gain_grad, gain_weight, gain_first, gain_second, inverse)
    return (
        velocity.astype(jnp.bfloat16),
        update,
        emb_new[0],
        emb_new[1],
        emb_new[2],
        gain_new[0],
        gain_new[1],
        gain_new[2],
    )


def solution(mesh):
    placed = (
        P(None, "shard", "tensor"),
        P(None, "shard", "tensor"),
        P(),
        P("shard", "tensor"),
        P("shard", "tensor"),
        P("shard", "tensor"),
        P("shard", "tensor"),
        P(("shard", "tensor")),
        P(("shard", "tensor")),
        P(("shard", "tensor")),
        P(("shard", "tensor")),
    )
    return jax.shard_map(
        body,
        mesh=mesh,
        in_specs=placed,
        out_specs=(
            P(None, "shard", "tensor"),
            P(None, "shard", "tensor"),
            P("shard", "tensor"),
            P("shard", "tensor"),
            P("shard", "tensor"),
            P(("shard", "tensor")),
            P(("shard", "tensor")),
            P(("shard", "tensor")),
        ),
        check_vma=False,
    )
```

```python
import functools
import math

import jax
import jax.numpy as jnp
from jax import lax
from jax.experimental import pallas as pl
from jax.experimental.pallas import tpu as pltpu
from jax.sharding import PartitionSpec as P

D = 2048
NS_STEPS = 4
CORES = 2
EDGE = 256
LIFT = 2.0**25
PACE = 2

linear_coef = 3.4445
cubic_coef = -4.775
quintic_coef = 2.0315
momentum_rate = 0.95
learn_rate = 0.01
decay_weight = 0.1
first_rate = 0.9
second_rate = 0.95
adam_floor = 1e-08
norm_floor = 1e-07


def adamw(grad, weight, first, second, inverse):
    scaled = grad * inverse
    first_new = first_rate * first + (1.0 - first_rate) * scaled
    second_new = second_rate * second + (1.0 - second_rate) * scaled * scaled
    weight_new = weight - learn_rate * (
        first_new / (jnp.sqrt(second_new) + adam_floor) + decay_weight * weight
    )
    return (weight_new, first_new, second_new)


def momentum_step(grads, momentum, inverse):
    scaled = grads * inverse
    velocity = momentum_rate * momentum.astype(jnp.float32) + scaled
    return velocity, scaled + momentum_rate * velocity


def span(index):
    return slice(index * EDGE, (index + 1) * EDGE)


def upper_blocks(width):
    return [(i, j) for j in range(width // EDGE) for i in range(j + 1)]


def write_gram(turned_ref, gram_ref):
    slot = 0
    for j in range(turned_ref.shape[0] // EDGE):
        part = lax.dot_general(
            turned_ref[: (j + 1) * EDGE, :],
            turned_ref[span(j), :],
            (((1,), (1,)), ((), ())),
            preferred_element_type=jnp.float32,
        )
        for i in range(j + 1):
            gram_ref[slot] = part[span(i), :].astype(jnp.bfloat16)
            slot += 1


def write_poly(own_ref, other_ref, gram, poly):
    for slot, (i, j) in enumerate(upper_blocks(gram.shape[0])):
        block = own_ref[slot].astype(jnp.float32) + other_ref[slot].astype(jnp.float32)
        block = block.astype(jnp.bfloat16)
        gram[span(i), span(j)] = block
        if i != j:
            gram[span(j), span(i)] = block.T
    for j in range(gram.shape[0] // EDGE):
        square = jnp.dot(
            gram[: (j + 1) * EDGE, :], gram[:, span(j)], preferred_element_type=jnp.float32
        )
        for i in range(j + 1):
            block = cubic_coef * gram[span(i), span(j)].astype(jnp.float32)
            block = (block + quintic_coef * square[span(i), :]).astype(jnp.bfloat16)
            poly[span(i), span(j)] = block
            if i != j:
                poly[span(j), span(i)] = block.T


def send_kernel(
    inverse_ref, grads_ref, momentum_ref, sent_ref, sums_ref, grads, momentum, sent, sems
):
    matrices, rows, cols = grads.shape
    parts = matrices // PACE
    arrivals, departures = [], []
    for p in range(parts):
        part = pl.ds(p * PACE, PACE)
        arrivals.append(
            [
                pltpu.make_async_copy(grads_ref.at[part], grads.at[part], sems.at[3 * p]),
                pltpu.make_async_copy(momentum_ref.at[part], momentum.at[part], sems.at[3 * p + 1]),
            ]
        )
        for copy in arrivals[-1]:
            copy.start()
    for p in range(parts):
        for copy in arrivals[p]:
            copy.wait()
        for k in range(p * PACE, (p + 1) * PACE):
            advance = momentum_step(grads[k], momentum[k], inverse_ref[0])[1]
            lifted = advance * LIFT
            sent[k] = ((lifted * lifted) * (lifted * jnp.abs(lifted))).astype(jnp.bfloat16)
            squares = (advance * advance).reshape(rows // 8, 8, cols).sum(axis=0)
            sums_ref[k] = sum(squares[:, c : c + 128] for c in range(0, cols, 128))
        part = pl.ds(p * PACE, PACE)
        departures.append(
            pltpu.make_async_copy(sent.at[part], sent_ref.at[part], sems.at[3 * p + 2])
        )
        departures[-1].start()
    for copy in departures:
        copy.wait()


def first_kernel(total_ref, block_ref, turned_ref, gram_ref, *, tensor):
    scale = 1.0 / (LIFT * (jnp.sqrt(jnp.full((1, 1), total_ref[0], jnp.float32)) + norm_floor))
    blocks, rows, cols = block_ref.shape
    for s in range(blocks // tensor):
        for t in range(tensor):
            power = block_ref[s * tensor + t].astype(jnp.float32)
            root = lax.rsqrt(lax.rsqrt(jnp.abs(power))) * scale
            iterate = jnp.where(power < 0.0, -root, root).astype(jnp.bfloat16)
            turned_ref[t * cols : (t + 1) * cols, s * rows : (s + 1) * rows] = iterate.T
    write_gram(turned_ref, gram_ref)


def middle_kernel(turned_ref, own_ref, other_ref, next_ref, gram_ref, gram, poly):
    write_poly(own_ref, other_ref, gram, poly)
    for c in range(turned_ref.shape[1] // EDGE):
        old = turned_ref[:, span(c)]
        new = linear_coef * old.astype(jnp.float32) + jnp.dot(
            poly[...], old, preferred_element_type=jnp.float32
        )
        next_ref[:, span(c)] = new.astype(jnp.bfloat16)
    write_gram(next_ref, gram_ref)


def last_kernel(
    turned_ref, own_ref, other_ref, block_ref, gram, poly, finished, sems, *, tensor, parts
):
    write_poly(own_ref, other_ref, gram, poly)
    blocks, rows, cols = block_ref.shape
    groups = blocks // tensor
    copies = []
    for s in range(groups):
        old = turned_ref[:, s * rows : (s + 1) * rows].T
        new = linear_coef * old.astype(jnp.float32) + jnp.dot(
            old, poly[...], preferred_element_type=jnp.float32
        )
        new = (math.sqrt(D) * new).astype(jnp.bfloat16)
        for t in range(tensor):
            finished[s * tensor + t] = new[:, t * cols : (t + 1) * cols]
        if (s + 1) % (groups // parts) == 0:
            part = pl.ds(len(copies) * (blocks // parts), blocks // parts)
            copies.append(
                pltpu.make_async_copy(
                    finished.at[part], block_ref.at[part], sems.at[len(copies)]
                )
            )
            copies[-1].start()
    for copy in copies:
        copy.wait()


limits = pltpu.CompilerParams(vmem_limit_bytes=16 * 2**20)
streamed = pltpu.CompilerParams(vmem_limit_bytes=60 * 2**20)


def run_kernel(kernel, results, scratch, *operands, out=pltpu.VMEM):
    whole = pl.BlockSpec(memory_space=pltpu.VMEM)
    scalar = pl.BlockSpec(memory_space=pltpu.SMEM)
    return pl.pallas_call(
        kernel,
        out_shape=results,
        in_specs=[scalar if value.ndim == 1 else whole for value in operands],
        out_specs=[pl.BlockSpec(memory_space=out)] * len(results),
        scratch_shapes=scratch,
        compiler_params=limits,
    )(*operands)


def code(grads, momentum, inverse):
    whole = pl.BlockSpec(memory_space=pl.ANY)
    sent, sums = pl.pallas_call(
        send_kernel,
        out_shape=[
            jax.ShapeDtypeStruct(grads.shape, jnp.bfloat16),
            jax.ShapeDtypeStruct((grads.shape[0], 8, 128), jnp.float32),
        ],
        in_specs=[pl.BlockSpec(memory_space=pltpu.SMEM), whole, whole],
        out_specs=[whole, pl.BlockSpec(memory_space=pltpu.VMEM)],
        scratch_shapes=[
            pltpu.VMEM(grads.shape, jnp.float32),
            pltpu.VMEM(grads.shape, jnp.bfloat16),
            pltpu.VMEM(grads.shape, jnp.bfloat16),
            pltpu.SemaphoreType.DMA((3 * grads.shape[0] // PACE,)),
        ],
        compiler_params=streamed,
    )(inverse.reshape(1), grads, momentum)
    return sent, jnp.sum(sums, axis=(1, 2))


def other_core(value):
    shards = lax.axis_size("shard")
    return lax.ppermute(value, "shard", [(i, i ^ 1) for i in range(shards)])


def chip_groups():
    shards, tensor = lax.axis_size("shard"), lax.axis_size("tensor")
    return [
        [s * tensor + t for s in range(core, shards, CORES) for t in range(tensor)]
        for core in range(CORES)
    ]


def exchange(blocks):
    return lax.all_to_all(
        blocks,
        ("shard", "tensor"),
        split_axis=0,
        concat_axis=0,
        axis_index_groups=chip_groups(),
        tiled=True,
    )


def orthogonalize(blocks, total):
    tensor = lax.axis_size("tensor")
    width = tensor * blocks.shape[2]
    height = blocks.shape[0] // tensor * blocks.shape[1]
    turned_type = jax.ShapeDtypeStruct((width, height), jnp.bfloat16)
    gram_type = jax.ShapeDtypeStruct((len(upper_blocks(width)), EDGE, EDGE), jnp.bfloat16)
    squares = [pltpu.VMEM((width, width), jnp.bfloat16)] * 2
    turned, own = run_kernel(
        functools.partial(first_kernel, tensor=tensor), [turned_type, gram_type], [], total, blocks
    )
    for _ in range(NS_STEPS - 1):
        turned, own = run_kernel(
            middle_kernel, [turned_type, gram_type], squares, turned, own, other_core(own)
        )
    parts = 4
    return run_kernel(
        functools.partial(last_kernel, tensor=tensor, parts=parts),
        [jax.ShapeDtypeStruct(blocks.shape, jnp.bfloat16)],
        squares + [pltpu.VMEM(blocks.shape, jnp.bfloat16), pltpu.SemaphoreType.DMA((parts,))],
        turned,
        own,
        other_core(own),
        out=pl.ANY,
    )[0]


def sum_over_devices(values):
    devices = lax.axis_size("shard") * lax.axis_size("tensor")
    bit = 1
    while bit < devices:
        pairs = [(i, i ^ bit) for i in range(devices)]
        values = values + lax.ppermute(values, ("shard", "tensor"), pairs)
        bit *= 2
    return values


def body(
    grads,
    momentum,
    counts,
    emb_grad,
    emb_weight,
    emb_first,
    emb_second,
    gain_grad,
    gain_weight,
    gain_first,
    gain_second,
):
    inverse = 1.0 / counts[0].astype(jnp.float32)
    sent, sums = code(grads, momentum, inverse)
    owned = exchange(sent)
    grads, momentum, _ = lax.optimization_barrier((grads, momentum, sent))
    velocity = momentum_step(grads, momentum, inverse)[0]
    chip = lax.axis_index("shard") // CORES * lax.axis_size("tensor") + lax.axis_index("tensor")
    total = lax.dynamic_slice_in_dim(sum_over_devices(sums), chip, 1)
    update = exchange(orthogonalize(owned, total)).astype(jnp.float32)
    emb_new = adamw(emb_grad, emb_weight, emb_first, emb_second, inverse)
    gain_new = adamw(gain_grad, gain_weight, gain_first, gain_second, inverse)
    return (
        velocity.astype(jnp.bfloat16),
        update,
        emb_new[0],
        emb_new[1],
        emb_new[2],
        gain_new[0],
        gain_new[1],
        gain_new[2],
    )


def solution(mesh):
    placed = (
        P(None, "shard", "tensor"),
        P(None, "shard", "tensor"),
        P(),
        P("shard", "tensor"),
        P("shard", "tensor"),
        P("shard", "tensor"),
        P("shard", "tensor"),
        P(("shard", "tensor")),
        P(("shard", "tensor")),
        P(("shard", "tensor")),
        P(("shard", "tensor")),
    )
    return jax.shard_map(
        body,
        mesh=mesh,
        in_specs=placed,
        out_specs=(
            P(None, "shard", "tensor"),
            P(None, "shard", "tensor"),
            P("shard", "tensor"),
            P("shard", "tensor"),
            P("shard", "tensor"),
            P(("shard", "tensor")),
            P(("shard", "tensor")),
            P(("shard", "tensor")),
        ),
        check_vma=False,
    )
```

```python
import functools
import math

import jax
import jax.numpy as jnp
from jax import lax
from jax.experimental import pallas as pl
from jax.experimental.pallas import tpu as pltpu
from jax.sharding import PartitionSpec as P

D = 2048
NS_STEPS = 4
CORES = 2
EDGE = 256
LIFT = 2.0**25
PARTS = 4
PACE = 2

linear_coef = 3.4445
cubic_coef = -4.775
quintic_coef = 2.0315
momentum_rate = 0.95
learn_rate = 0.01
decay_weight = 0.1
first_rate = 0.9
second_rate = 0.95
adam_floor = 1e-08
norm_floor = 1e-07


def adamw(grad, weight, first, second, inverse):
    scaled = grad * inverse
    first_new = first_rate * first + (1.0 - first_rate) * scaled
    second_new = second_rate * second + (1.0 - second_rate) * scaled * scaled
    weight_new = weight - learn_rate * (
        first_new / (jnp.sqrt(second_new) + adam_floor) + decay_weight * weight
    )
    return (weight_new, first_new, second_new)


def span(index):
    return slice(index * EDGE, (index + 1) * EDGE)


def upper_blocks(width):
    return [(i, j) for j in range(width // EDGE) for i in range(j + 1)]


def write_gram(turned_ref, gram_ref):
    slot = 0
    for j in range(turned_ref.shape[0] // EDGE):
        part = lax.dot_general(
            turned_ref[: (j + 1) * EDGE, :],
            turned_ref[span(j), :],
            (((1,), (1,)), ((), ())),
            preferred_element_type=jnp.float32,
        )
        for i in range(j + 1):
            gram_ref[slot] = part[span(i), :].astype(jnp.bfloat16)
            slot += 1


def symmetric(left, right, finish, out):
    for j in range(out.shape[0] // EDGE):
        product = jnp.dot(
            left[: (j + 1) * EDGE, :], right[:, span(j)], preferred_element_type=jnp.float32
        )
        for i in range(j + 1):
            place = (span(i), span(j))
            block = finish(place, product[span(i), :]).astype(jnp.bfloat16)
            out[place] = block
            if i != j:
                out[span(j), span(i)] = block.T


def write_factor(own_ref, other_ref, gram, poly, spare, later):
    def read(ref, place):
        return ref[place].astype(jnp.float32)

    def polynomial(grams, out):
        symmetric(
            grams,
            grams,
            lambda place, square: cubic_coef * read(grams, place) + quintic_coef * square,
            out,
        )

    for slot, (i, j) in enumerate(upper_blocks(gram.shape[0])):
        block = own_ref[slot].astype(jnp.float32) + other_ref[slot].astype(jnp.float32)
        block = block.astype(jnp.bfloat16)
        gram[span(i), span(j)] = block
        if i != j:
            gram[span(j), span(i)] = block.T
    polynomial(gram, poly)
    symmetric(
        poly, poly, lambda place, square: 2.0 * linear_coef * read(poly, place) + square, spare
    )
    symmetric(
        gram, spare, lambda place, change: linear_coef**2 * read(gram, place) + change, later
    )
    polynomial(later, gram)
    symmetric(
        poly,
        gram,
        lambda place, both: linear_coef * (read(poly, place) + read(gram, place)) + both,
        spare,
    )


def send_kernel(
    inverse_ref, grads_ref, momentum_ref, sent_ref, sums_ref, grads, momentum, sent, sems
):
    grad_part = LIFT * (1.0 + momentum_rate) * inverse_ref[0]
    momentum_part = LIFT * momentum_rate**2
    matrices, rows, cols = grads.shape
    parts = matrices // PACE
    arrivals, departures = [], []
    for p in range(parts):
        part = pl.ds(p * PACE, PACE)
        arrivals.append(
            [
                pltpu.make_async_copy(grads_ref.at[part], grads.at[part], sems.at[3 * p]),
                pltpu.make_async_copy(momentum_ref.at[part], momentum.at[part], sems.at[3 * p + 1]),
            ]
        )
        for copy in arrivals[-1]:
            copy.start()
    for p in range(parts):
        for copy in arrivals[p]:
            copy.wait()
        for k in range(p * PACE, (p + 1) * PACE):
            lifted = grad_part * grads[k] + momentum_part * momentum[k].astype(jnp.float32)
            squares = lifted * lifted
            sent[k] = (squares * (lifted * jnp.abs(lifted))).astype(jnp.bfloat16)
            squares = squares.reshape(rows // 8, 8, cols).sum(axis=0)
            sums_ref[k] = sum(squares[:, c : c + 128] for c in range(0, cols, 128))
        part = pl.ds(p * PACE, PACE)
        departures.append(
            pltpu.make_async_copy(sent.at[part], sent_ref.at[part], sems.at[3 * p + 2])
        )
        departures[-1].start()
    for copy in departures:
        copy.wait()


def first_kernel(totals_ref, chip_ref, block_ref, turned_ref, gram_ref, *, tensor):
    scale = 1.0 / (jnp.sqrt(jnp.full((1, 1), totals_ref[chip_ref[0]], jnp.float32)) + LIFT * norm_floor)
    blocks, rows, cols = block_ref.shape
    for s in range(blocks // tensor):
        for t in range(tensor):
            power = block_ref[s * tensor + t].astype(jnp.float32)
            root = lax.rsqrt(lax.rsqrt(jnp.abs(power))) * scale
            iterate = jnp.where(power < 0.0, -root, root).astype(jnp.bfloat16)
            turned_ref[t * cols : (t + 1) * cols, s * rows : (s + 1) * rows] = iterate.T
    write_gram(turned_ref, gram_ref)


def middle_kernel(turned_ref, own_ref, other_ref, next_ref, gram_ref, *squares):
    write_factor(own_ref, other_ref, *squares)
    factor = squares[2]
    for c in range(turned_ref.shape[1] // EDGE):
        old = turned_ref[:, span(c)]
        new = linear_coef**2 * old.astype(jnp.float32) + jnp.dot(
            factor[...], old, preferred_element_type=jnp.float32
        )
        next_ref[:, span(c)] = new.astype(jnp.bfloat16)
    write_gram(next_ref, gram_ref)


def last_kernel(turned_ref, own_ref, other_ref, block_ref, finished, sems, *squares, tensor):
    write_factor(own_ref, other_ref, *squares)
    factor = squares[2]
    blocks, rows, cols = block_ref.shape
    groups = blocks // tensor
    copies = []
    for s in range(groups):
        old = turned_ref[:, s * rows : (s + 1) * rows].T
        new = linear_coef**2 * old.astype(jnp.float32) + jnp.dot(
            old, factor[...], preferred_element_type=jnp.float32
        )
        new = (math.sqrt(D) * new).astype(jnp.bfloat16)
        for t in range(tensor):
            finished[s * tensor + t] = new[:, t * cols : (t + 1) * cols]
        if (s + 1) % (groups // PARTS) == 0:
            part = pl.ds(len(copies) * (blocks // PARTS), blocks // PARTS)
            copies.append(
                pltpu.make_async_copy(
                    finished.at[part], block_ref.at[part], sems.at[len(copies)]
                )
            )
            copies[-1].start()
    for copy in copies:
        copy.wait()


limits = pltpu.CompilerParams(vmem_limit_bytes=20 * 2**20)
streamed = pltpu.CompilerParams(vmem_limit_bytes=60 * 2**20)


def run_kernel(kernel, results, scratch, *operands, out=pltpu.VMEM):
    whole = pl.BlockSpec(memory_space=pltpu.VMEM)
    scalar = pl.BlockSpec(memory_space=pltpu.SMEM)
    return pl.pallas_call(
        kernel,
        out_shape=results,
        in_specs=[scalar if value.ndim == 1 else whole for value in operands],
        out_specs=[pl.BlockSpec(memory_space=out)] * len(results),
        scratch_shapes=scratch,
        compiler_params=limits,
    )(*operands)


def code(grads, momentum, inverse):
    whole = pl.BlockSpec(memory_space=pl.ANY)
    sent, sums = pl.pallas_call(
        send_kernel,
        out_shape=[
            jax.ShapeDtypeStruct(grads.shape, jnp.bfloat16),
            jax.ShapeDtypeStruct((grads.shape[0], 8, 128), jnp.float32),
        ],
        in_specs=[pl.BlockSpec(memory_space=pltpu.SMEM), whole, whole],
        out_specs=[whole, pl.BlockSpec(memory_space=pltpu.VMEM)],
        scratch_shapes=[
            pltpu.VMEM(grads.shape, jnp.float32),
            pltpu.VMEM(grads.shape, jnp.bfloat16),
            pltpu.VMEM(grads.shape, jnp.bfloat16),
            pltpu.SemaphoreType.DMA((3 * grads.shape[0] // PACE,)),
        ],
        compiler_params=streamed,
    )(inverse.reshape(1), grads, momentum)
    return sent, jnp.sum(sums, axis=(1, 2))


def other_core(value):
    shards = lax.axis_size("shard")
    return lax.ppermute(value, "shard", [(i, i ^ 1) for i in range(shards)])


def chip_groups():
    shards, tensor = lax.axis_size("shard"), lax.axis_size("tensor")
    return [
        [s * tensor + t for s in range(core, shards, CORES) for t in range(tensor)]
        for core in range(CORES)
    ]


def exchange(blocks):
    return lax.all_to_all(
        blocks,
        ("shard", "tensor"),
        split_axis=0,
        concat_axis=0,
        axis_index_groups=chip_groups(),
        tiled=True,
    )


def orthogonalize(blocks, totals):
    tensor = lax.axis_size("tensor")
    chip = (lax.axis_index("shard") // CORES * tensor + lax.axis_index("tensor")).reshape(1)
    width = tensor * blocks.shape[2]
    height = blocks.shape[0] // tensor * blocks.shape[1]
    turned_type = jax.ShapeDtypeStruct((width, height), jnp.bfloat16)
    gram_type = jax.ShapeDtypeStruct((len(upper_blocks(width)), EDGE, EDGE), jnp.bfloat16)
    squares = [pltpu.VMEM((width, width), jnp.bfloat16)] * 4
    turned, own = run_kernel(
        functools.partial(first_kernel, tensor=tensor), [turned_type, gram_type], [], totals, chip, blocks
    )
    for _ in range(NS_STEPS // 2 - 1):
        turned, own = run_kernel(
            middle_kernel, [turned_type, gram_type], squares, turned, own, other_core(own)
        )
    return run_kernel(
        functools.partial(last_kernel, tensor=tensor),
        [jax.ShapeDtypeStruct(blocks.shape, jnp.bfloat16)],
        [pltpu.VMEM(blocks.shape, jnp.bfloat16), pltpu.SemaphoreType.DMA((PARTS,))] + squares,
        turned,
        own,
        other_core(own),
        out=pl.ANY,
    )[0]


def sum_over_devices(values):
    devices = lax.axis_size("shard") * lax.axis_size("tensor")
    bit = 1
    while bit < devices:
        pairs = [(i, i ^ bit) for i in range(devices)]
        values = values + lax.ppermute(values, ("shard", "tensor"), pairs)
        bit *= 2
    return values


def body(
    grads,
    momentum,
    counts,
    emb_grad,
    emb_weight,
    emb_first,
    emb_second,
    gain_grad,
    gain_weight,
    gain_first,
    gain_second,
):
    inverse = 1.0 / counts[0].astype(jnp.float32)
    sent, sums = code(grads, momentum, inverse)
    owned = exchange(sent)
    grads, momentum, _ = lax.optimization_barrier((grads, momentum, sent))
    velocity = momentum_rate * momentum.astype(jnp.float32) + grads * inverse
    update = exchange(orthogonalize(owned, sum_over_devices(sums))).astype(jnp.float32)
    emb_new = adamw(emb_grad, emb_weight, emb_first, emb_second, inverse)
    gain_new = adamw(gain_grad, gain_weight, gain_first, gain_second, inverse)
    return (
        velocity.astype(jnp.bfloat16),
        update,
        emb_new[0],
        emb_new[1],
        emb_new[2],
        gain_new[0],
        gain_new[1],
        gain_new[2],
    )


def solution(mesh):
    placed = (
        P(None, "shard", "tensor"),
        P(None, "shard", "tensor"),
        P(),
        P("shard", "tensor"),
        P("shard", "tensor"),
        P("shard", "tensor"),
        P("shard", "tensor"),
        P(("shard", "tensor")),
        P(("shard", "tensor")),
        P(("shard", "tensor")),
        P(("shard", "tensor")),
    )
    return jax.shard_map(
        body,
        mesh=mesh,
        in_specs=placed,
        out_specs=(
            P(None, "shard", "tensor"),
            P(None, "shard", "tensor"),
            P("shard", "tensor"),
            P("shard", "tensor"),
            P("shard", "tensor"),
            P(("shard", "tensor")),
            P(("shard", "tensor")),
            P(("shard", "tensor")),
        ),
        check_vma=False,
    )
```

```python
import functools
import math

import jax
import jax.numpy as jnp
from jax import lax
from jax.experimental import pallas as pl
from jax.experimental.pallas import tpu as pltpu
from jax.sharding import PartitionSpec as P

D = 2048
NS_STEPS = 4
CORES = 2
EDGE = 256
LIFT = 2.0**25
PARTS = 4
PACE = 2

linear_coef = 3.4445
cubic_coef = -4.775
quintic_coef = 2.0315
momentum_rate = 0.95
learn_rate = 0.01
decay_weight = 0.1
first_rate = 0.9
second_rate = 0.95
adam_floor = 1e-08
norm_floor = 1e-07


def adamw(grad, weight, first, second, inverse):
    scaled = grad * inverse
    first_new = first_rate * first + (1.0 - first_rate) * scaled
    second_new = second_rate * second + (1.0 - second_rate) * scaled * scaled
    weight_new = weight - learn_rate * (
        first_new / (jnp.sqrt(second_new) + adam_floor) + decay_weight * weight
    )
    return (weight_new, first_new, second_new)


def span(index):
    return slice(index * EDGE, (index + 1) * EDGE)


def upper_blocks(width):
    return [(i, j) for j in range(width // EDGE) for i in range(j + 1)]


def write_gram(turned_ref, gram_ref):
    slot = 0
    for j in range(turned_ref.shape[0] // EDGE):
        part = lax.dot_general(
            turned_ref[: (j + 1) * EDGE, :],
            turned_ref[span(j), :],
            (((1,), (1,)), ((), ())),
            preferred_element_type=jnp.float32,
        )
        for i in range(j + 1):
            gram_ref[slot] = part[span(i), :].astype(jnp.bfloat16)
            slot += 1


def symmetric(left, right, finish, out):
    for j in reversed(range(out.shape[0] // EDGE)):
        product = jnp.dot(
            left[: (j + 1) * EDGE, :], right[:, span(j)], preferred_element_type=jnp.float32
        )
        for i in range(j + 1):
            place = (span(i), span(j))
            block = finish(place, product[span(i), :]).astype(jnp.bfloat16)
            out[place] = block
            if i != j:
                out[span(j), span(i)] = block.T


def write_factor(own_ref, other_ref, gram, poly, spare, later):
    def read(ref, place):
        return ref[place].astype(jnp.float32)

    def polynomial(grams, out):
        symmetric(
            grams,
            grams,
            lambda place, square: cubic_coef * read(grams, place) + quintic_coef * square,
            out,
        )

    for slot, (i, j) in enumerate(upper_blocks(gram.shape[0])):
        block = own_ref[slot].astype(jnp.float32) + other_ref[slot].astype(jnp.float32)
        block = block.astype(jnp.bfloat16)
        gram[span(i), span(j)] = block
        if i != j:
            gram[span(j), span(i)] = block.T
    polynomial(gram, poly)
    symmetric(
        poly, poly, lambda place, square: 2.0 * linear_coef * read(poly, place) + square, spare
    )
    symmetric(
        gram, spare, lambda place, change: linear_coef**2 * read(gram, place) + change, later
    )
    polynomial(later, gram)
    symmetric(
        poly,
        gram,
        lambda place, both: linear_coef * (read(poly, place) + read(gram, place)) + both,
        spare,
    )


def send_kernel(
    inverse_ref, grads_ref, momentum_ref, sent_ref, sums_ref, grads, momentum, sent, sems
):
    grad_part = LIFT * (1.0 + momentum_rate) * inverse_ref[0]
    momentum_part = LIFT * momentum_rate**2
    matrices, rows, cols = grads.shape
    parts = matrices // PACE
    arrivals, departures = [], []
    for p in range(parts):
        part = pl.ds(p * PACE, PACE)
        arrivals.append(
            [
                pltpu.make_async_copy(grads_ref.at[part], grads.at[part], sems.at[3 * p]),
                pltpu.make_async_copy(momentum_ref.at[part], momentum.at[part], sems.at[3 * p + 1]),
            ]
        )
        for copy in arrivals[-1]:
            copy.start()
    for p in range(parts):
        for copy in arrivals[p]:
            copy.wait()
        for k in range(p * PACE, (p + 1) * PACE):
            lifted = grad_part * grads[k] + momentum_part * momentum[k].astype(jnp.float32)
            squares = lifted * lifted
            sent[k] = (squares * (lifted * jnp.abs(lifted))).astype(jnp.bfloat16)
            squares = squares.reshape(rows // 8, 8, cols).sum(axis=0)
            sums_ref[k] = sum(squares[:, c : c + 128] for c in range(0, cols, 128))
        part = pl.ds(p * PACE, PACE)
        departures.append(
            pltpu.make_async_copy(sent.at[part], sent_ref.at[part], sems.at[3 * p + 2])
        )
        departures[-1].start()
    for copy in departures:
        copy.wait()


def first_kernel(totals_ref, chip_ref, block_ref, turned_ref, gram_ref, *, tensor):
    scale = 1.0 / (jnp.sqrt(jnp.full((1, 1), totals_ref[chip_ref[0]], jnp.float32)) + LIFT * norm_floor)
    blocks, rows, cols = block_ref.shape
    for s in range(blocks // tensor):
        for t in range(tensor):
            power = block_ref[s * tensor + t].astype(jnp.float32)
            root = lax.rsqrt(lax.rsqrt(jnp.abs(power))) * scale
            iterate = jnp.where(power < 0.0, -root, root).astype(jnp.bfloat16)
            turned_ref[t * cols : (t + 1) * cols, s * rows : (s + 1) * rows] = iterate.T
    write_gram(turned_ref, gram_ref)


def middle_kernel(turned_ref, own_ref, other_ref, next_ref, gram_ref, *squares):
    write_factor(own_ref, other_ref, *squares)
    factor = squares[2]
    for c in range(turned_ref.shape[1] // EDGE):
        old = turned_ref[:, span(c)]
        new = linear_coef**2 * old.astype(jnp.float32) + jnp.dot(
            factor[...], old, preferred_element_type=jnp.float32
        )
        next_ref[:, span(c)] = new.astype(jnp.bfloat16)
    write_gram(next_ref, gram_ref)


def last_kernel(turned_ref, own_ref, other_ref, block_ref, finished, sems, *squares, tensor):
    write_factor(own_ref, other_ref, *squares)
    factor = squares[2]
    blocks, rows, cols = block_ref.shape
    groups = blocks // tensor
    copies = []
    for s in range(groups):
        old = turned_ref[:, s * rows : (s + 1) * rows].T
        new = linear_coef**2 * old.astype(jnp.float32) + jnp.dot(
            old, factor[...], preferred_element_type=jnp.float32
        )
        new = (math.sqrt(D) * new).astype(jnp.bfloat16)
        for t in range(tensor):
            finished[s * tensor + t] = new[:, t * cols : (t + 1) * cols]
        if (s + 1) % (groups // PARTS) == 0:
            part = pl.ds(len(copies) * (blocks // PARTS), blocks // PARTS)
            copies.append(
                pltpu.make_async_copy(
                    finished.at[part], block_ref.at[part], sems.at[len(copies)]
                )
            )
            copies[-1].start()
    for copy in copies:
        copy.wait()


limits = pltpu.CompilerParams(vmem_limit_bytes=20 * 2**20)
streamed = pltpu.CompilerParams(vmem_limit_bytes=60 * 2**20)


def run_kernel(kernel, results, scratch, *operands, out=pltpu.VMEM):
    whole = pl.BlockSpec(memory_space=pltpu.VMEM)
    scalar = pl.BlockSpec(memory_space=pltpu.SMEM)
    return pl.pallas_call(
        kernel,
        out_shape=results,
        in_specs=[scalar if value.ndim == 1 else whole for value in operands],
        out_specs=[pl.BlockSpec(memory_space=out)] * len(results),
        scratch_shapes=scratch,
        compiler_params=limits,
    )(*operands)


def code(grads, momentum, inverse):
    whole = pl.BlockSpec(memory_space=pl.ANY)
    sent, sums = pl.pallas_call(
        send_kernel,
        out_shape=[
            jax.ShapeDtypeStruct(grads.shape, jnp.bfloat16),
            jax.ShapeDtypeStruct((grads.shape[0], 8, 128), jnp.float32),
        ],
        in_specs=[pl.BlockSpec(memory_space=pltpu.SMEM), whole, whole],
        out_specs=[whole, pl.BlockSpec(memory_space=pltpu.VMEM)],
        scratch_shapes=[
            pltpu.VMEM(grads.shape, jnp.float32),
            pltpu.VMEM(grads.shape, jnp.bfloat16),
            pltpu.VMEM(grads.shape, jnp.bfloat16),
            pltpu.SemaphoreType.DMA((3 * grads.shape[0] // PACE,)),
        ],
        compiler_params=streamed,
    )(inverse.reshape(1), grads, momentum)
    return sent, jnp.sum(sums, axis=(1, 2))


def other_core(value):
    shards = lax.axis_size("shard")
    return lax.ppermute(value, "shard", [(i, i ^ 1) for i in range(shards)])


def chip_groups():
    shards, tensor = lax.axis_size("shard"), lax.axis_size("tensor")
    return [
        [s * tensor + t for s in range(core, shards, CORES) for t in range(tensor)]
        for core in range(CORES)
    ]


def exchange(blocks):
    return lax.all_to_all(
        blocks,
        ("shard", "tensor"),
        split_axis=0,
        concat_axis=0,
        axis_index_groups=chip_groups(),
        tiled=True,
    )


def orthogonalize(blocks, totals):
    tensor = lax.axis_size("tensor")
    chip = (lax.axis_index("shard") // CORES * tensor + lax.axis_index("tensor")).reshape(1)
    width = tensor * blocks.shape[2]
    height = blocks.shape[0] // tensor * blocks.shape[1]
    turned_type = jax.ShapeDtypeStruct((width, height), jnp.bfloat16)
    gram_type = jax.ShapeDtypeStruct((len(upper_blocks(width)), EDGE, EDGE), jnp.bfloat16)
    squares = [pltpu.VMEM((width, width), jnp.bfloat16)] * 4
    turned, own = run_kernel(
        functools.partial(first_kernel, tensor=tensor), [turned_type, gram_type], [], totals, chip, blocks
    )
    for _ in range(NS_STEPS // 2 - 1):
        turned, own = run_kernel(
            middle_kernel, [turned_type, gram_type], squares, turned, own, other_core(own)
        )
    return run_kernel(
        functools.partial(last_kernel, tensor=tensor),
        [jax.ShapeDtypeStruct(blocks.shape, jnp.bfloat16)],
        [pltpu.VMEM(blocks.shape, jnp.bfloat16), pltpu.SemaphoreType.DMA((PARTS,))] + squares,
        turned,
        own,
        other_core(own),
        out=pl.ANY,
    )[0]


def sum_over_devices(values):
    devices = lax.axis_size("shard") * lax.axis_size("tensor")
    bit = 1
    while bit < devices:
        pairs = [(i, i ^ bit) for i in range(devices)]
        values = values + lax.ppermute(values, ("shard", "tensor"), pairs)
        bit *= 2
    return values


def body(
    grads,
    momentum,
    counts,
    emb_grad,
    emb_weight,
    emb_first,
    emb_second,
    gain_grad,
    gain_weight,
    gain_first,
    gain_second,
):
    inverse = 1.0 / counts[0].astype(jnp.float32)
    sent, sums = code(grads, momentum, inverse)
    owned = exchange(sent)
    grads, momentum, _ = lax.optimization_barrier((grads, momentum, sent))
    velocity = momentum_rate * momentum.astype(jnp.float32) + grads * inverse
    update = exchange(orthogonalize(owned, sum_over_devices(sums))).astype(jnp.float32)
    emb_new = adamw(emb_grad, emb_weight, emb_first, emb_second, inverse)
    gain_new = adamw(gain_grad, gain_weight, gain_first, gain_second, inverse)
    return (
        velocity.astype(jnp.bfloat16),
        update,
        emb_new[0],
        emb_new[1],
        emb_new[2],
        gain_new[0],
        gain_new[1],
        gain_new[2],
    )


def solution(mesh):
    placed = (
        P(None, "shard", "tensor"),
        P(None, "shard", "tensor"),
        P(),
        P("shard", "tensor"),
        P("shard", "tensor"),
        P("shard", "tensor"),
        P("shard", "tensor"),
        P(("shard", "tensor")),
        P(("shard", "tensor")),
        P(("shard", "tensor")),
        P(("shard", "tensor")),
    )
    return jax.shard_map(
        body,
        mesh=mesh,
        in_specs=placed,
        out_specs=(
            P(None, "shard", "tensor"),
            P(None, "shard", "tensor"),
            P("shard", "tensor"),
            P("shard", "tensor"),
            P("shard", "tensor"),
            P(("shard", "tensor")),
            P(("shard", "tensor")),
            P(("shard", "tensor")),
        ),
        check_vma=False,
    )
```

```python
import functools
import math

import jax
import jax.numpy as jnp
from jax import lax
from jax.experimental import pallas as pl
from jax.experimental.pallas import tpu as pltpu
from jax.sharding import PartitionSpec as P

D = 2048
NS_STEPS = 4
CORES = 2
EDGE = 256
LIFT = 2.0**25
PARTS = 4
PACE = 2

linear_coef = 3.4445
cubic_coef = -4.775
quintic_coef = 2.0315
momentum_rate = 0.95
learn_rate = 0.01
decay_weight = 0.1
first_rate = 0.9
second_rate = 0.95
adam_floor = 1e-08
norm_floor = 1e-07


def adamw(grad, weight, first, second, inverse):
    scaled = grad * inverse
    first_new = first_rate * first + (1.0 - first_rate) * scaled
    second_new = second_rate * second + (1.0 - second_rate) * scaled * scaled
    weight_new = weight - learn_rate * (
        first_new / (jnp.sqrt(second_new) + adam_floor) + decay_weight * weight
    )
    return (weight_new, first_new, second_new)


def span(index):
    return slice(index * EDGE, (index + 1) * EDGE)


def upper_blocks(width):
    return [(i, j) for j in range(width // EDGE) for i in range(j + 1)]


def write_gram(turned_ref, gram_ref):
    for j in reversed(range(turned_ref.shape[0] // EDGE)):
        part = lax.dot_general(
            turned_ref[: (j + 1) * EDGE, :],
            turned_ref[span(j), :],
            (((1,), (1,)), ((), ())),
            preferred_element_type=jnp.float32,
        )
        for i in range(j + 1):
            gram_ref[j * (j + 1) // 2 + i] = part[span(i), :].astype(jnp.bfloat16)


def symmetric(left, right, finish, out):
    for j in reversed(range(out.shape[0] // EDGE)):
        product = jnp.dot(
            left[: (j + 1) * EDGE, :], right[:, span(j)], preferred_element_type=jnp.float32
        )
        for i in range(j + 1):
            place = (span(i), span(j))
            block = finish(place, product[span(i), :]).astype(jnp.bfloat16)
            out[place] = block
            if i != j:
                out[span(j), span(i)] = block.T


def write_factor(own_ref, other_ref, gram, poly, spare, later):
    def read(ref, place):
        return ref[place].astype(jnp.float32)

    def polynomial(grams, out):
        symmetric(
            grams,
            grams,
            lambda place, square: cubic_coef * read(grams, place) + quintic_coef * square,
            out,
        )

    for slot, (i, j) in enumerate(upper_blocks(gram.shape[0])):
        block = own_ref[slot].astype(jnp.float32) + other_ref[slot].astype(jnp.float32)
        block = block.astype(jnp.bfloat16)
        gram[span(i), span(j)] = block
        if i != j:
            gram[span(j), span(i)] = block.T
    polynomial(gram, poly)
    symmetric(
        poly, poly, lambda place, square: 2.0 * linear_coef * read(poly, place) + square, spare
    )
    symmetric(
        gram, spare, lambda place, change: linear_coef**2 * read(gram, place) + change, later
    )
    polynomial(later, gram)
    symmetric(
        poly,
        gram,
        lambda place, both: linear_coef * (read(poly, place) + read(gram, place)) + both,
        spare,
    )


def send_kernel(
    inverse_ref, grads_ref, momentum_ref, sent_ref, sums_ref, grads, momentum, sems
):
    grad_part = LIFT * (1.0 + momentum_rate) * inverse_ref[0]
    momentum_part = LIFT * momentum_rate**2
    matrices, rows, cols = grads.shape
    parts = matrices // PACE
    arrivals = []
    for p in range(parts):
        part = pl.ds(p * PACE, PACE)
        arrivals.append(
            [
                pltpu.make_async_copy(grads_ref.at[part], grads.at[part], sems.at[2 * p]),
                pltpu.make_async_copy(momentum_ref.at[part], momentum.at[part], sems.at[2 * p + 1]),
            ]
        )
        for copy in arrivals[-1]:
            copy.start()
    for p in range(parts):
        for copy in arrivals[p]:
            copy.wait()
        for k in range(p * PACE, (p + 1) * PACE):
            lifted = grad_part * grads[k] + momentum_part * momentum[k].astype(jnp.float32)
            squares = lifted * lifted
            sent_ref[k] = (squares * (lifted * jnp.abs(lifted))).astype(jnp.bfloat16)
            squares = squares.reshape(rows // 8, 8, cols).sum(axis=0)
            sums_ref[k] = sum(squares[:, c : c + 128] for c in range(0, cols, 128))


def first_kernel(totals_ref, chip_ref, block_ref, turned_ref, gram_ref, *, tensor):
    scale = 1.0 / (jnp.sqrt(jnp.full((1, 1), totals_ref[chip_ref[0]], jnp.float32)) + LIFT * norm_floor)
    blocks, rows, cols = block_ref.shape
    for s in range(blocks // tensor):
        for t in range(tensor):
            power = block_ref[s * tensor + t].T.astype(jnp.float32)
            root = lax.rsqrt(lax.rsqrt(jnp.abs(power))) * scale
            iterate = jnp.where(power < 0.0, -root, root).astype(jnp.bfloat16)
            turned_ref[t * cols : (t + 1) * cols, s * rows : (s + 1) * rows] = iterate
    write_gram(turned_ref, gram_ref)


def middle_kernel(turned_ref, own_ref, other_ref, next_ref, gram_ref, *squares):
    write_factor(own_ref, other_ref, *squares)
    factor = squares[2]
    for c in range(turned_ref.shape[0] // EDGE):
        new = linear_coef**2 * turned_ref[span(c), :].astype(jnp.float32) + jnp.dot(
            factor[span(c), :], turned_ref[...], preferred_element_type=jnp.float32
        )
        next_ref[span(c), :] = new.astype(jnp.bfloat16)
    write_gram(next_ref, gram_ref)


def flip_kernel(turned_ref, straight_ref):
    for c in range(turned_ref.shape[1] // EDGE):
        straight_ref[span(c), :] = turned_ref[:, span(c)].T


def last_kernel(straight_ref, own_ref, other_ref, block_ref, finished, sems, *squares, tensor):
    write_factor(own_ref, other_ref, *squares)
    factor = squares[2]
    blocks, rows, cols = block_ref.shape
    groups = blocks // tensor
    copies = []
    for s in range(groups):
        old = straight_ref[s * rows : (s + 1) * rows, :]
        new = linear_coef**2 * old.astype(jnp.float32) + jnp.dot(
            old, factor[...], preferred_element_type=jnp.float32
        )
        new = (math.sqrt(D) * new).astype(jnp.bfloat16)
        for t in range(tensor):
            finished[s * tensor + t] = new[:, t * cols : (t + 1) * cols]
        if (s + 1) % (groups // PARTS) == 0:
            part = pl.ds(len(copies) * (blocks // PARTS), blocks // PARTS)
            copies.append(
                pltpu.make_async_copy(
                    finished.at[part], block_ref.at[part], sems.at[len(copies)]
                )
            )
            copies[-1].start()
    for copy in copies:
        copy.wait()


limits = pltpu.CompilerParams(vmem_limit_bytes=20 * 2**20)
streamed = pltpu.CompilerParams(vmem_limit_bytes=60 * 2**20)


def run_kernel(kernel, results, scratch, *operands, out=pltpu.VMEM):
    whole = pl.BlockSpec(memory_space=pltpu.VMEM)
    scalar = pl.BlockSpec(memory_space=pltpu.SMEM)
    return pl.pallas_call(
        kernel,
        out_shape=results,
        in_specs=[scalar if value.ndim == 1 else whole for value in operands],
        out_specs=[pl.BlockSpec(memory_space=out)] * len(results),
        scratch_shapes=scratch,
        compiler_params=limits,
    )(*operands)


def code(grads, momentum, inverse):
    whole = pl.BlockSpec(memory_space=pl.ANY)
    sent, sums = pl.pallas_call(
        send_kernel,
        out_shape=[
            jax.ShapeDtypeStruct(grads.shape, jnp.bfloat16),
            jax.ShapeDtypeStruct((grads.shape[0], 8, 128), jnp.float32),
        ],
        in_specs=[pl.BlockSpec(memory_space=pltpu.SMEM), whole, whole],
        out_specs=[pl.BlockSpec(memory_space=pltpu.VMEM)] * 2,
        scratch_shapes=[
            pltpu.VMEM(grads.shape, jnp.float32),
            pltpu.VMEM(grads.shape, jnp.bfloat16),
            pltpu.SemaphoreType.DMA((2 * grads.shape[0] // PACE,)),
        ],
        compiler_params=streamed,
    )(inverse.reshape(1), grads, momentum)
    return sent, jnp.sum(sums, axis=(1, 2))


def other_core(value):
    shards = lax.axis_size("shard")
    return lax.ppermute(value, "shard", [(i, i ^ 1) for i in range(shards)])


def chip_groups():
    shards, tensor = lax.axis_size("shard"), lax.axis_size("tensor")
    return [
        [s * tensor + t for s in range(core, shards, CORES) for t in range(tensor)]
        for core in range(CORES)
    ]


def exchange(blocks):
    return lax.all_to_all(
        blocks,
        ("shard", "tensor"),
        split_axis=0,
        concat_axis=0,
        axis_index_groups=chip_groups(),
        tiled=True,
    )


def orthogonalize(blocks, totals):
    tensor = lax.axis_size("tensor")
    chip = (lax.axis_index("shard") // CORES * tensor + lax.axis_index("tensor")).reshape(1)
    width = tensor * blocks.shape[2]
    height = blocks.shape[0] // tensor * blocks.shape[1]
    turned_type = jax.ShapeDtypeStruct((width, height), jnp.bfloat16)
    gram_type = jax.ShapeDtypeStruct((len(upper_blocks(width)), EDGE, EDGE), jnp.bfloat16)
    squares = [pltpu.VMEM((width, width), jnp.bfloat16)] * 4
    turned, own = run_kernel(
        functools.partial(first_kernel, tensor=tensor), [turned_type, gram_type], [], totals, chip, blocks
    )
    for _ in range(NS_STEPS // 2 - 1):
        turned, own = run_kernel(
            middle_kernel, [turned_type, gram_type], squares, turned, own, other_core(own)
        )
    straight_type = jax.ShapeDtypeStruct((height, width), jnp.bfloat16)
    straight = run_kernel(flip_kernel, [straight_type], [], turned)[0]
    return run_kernel(
        functools.partial(last_kernel, tensor=tensor),
        [jax.ShapeDtypeStruct(blocks.shape, jnp.bfloat16)],
        [pltpu.VMEM(blocks.shape, jnp.bfloat16), pltpu.SemaphoreType.DMA((PARTS,))] + squares,
        straight,
        own,
        other_core(own),
        out=pl.ANY,
    )[0]


def sum_over_devices(values):
    devices = lax.axis_size("shard") * lax.axis_size("tensor")
    bits = [1 << k for k in range(devices.bit_length() - 1)]
    bits[-1] += bits[-2]
    for bit in bits:
        pairs = [(i, i ^ bit) for i in range(devices)]
        values = values + lax.ppermute(values, ("shard", "tensor"), pairs)
    return values


def body(
    grads,
    momentum,
    counts,
    emb_grad,
    emb_weight,
    emb_first,
    emb_second,
    gain_grad,
    gain_weight,
    gain_first,
    gain_second,
):
    inverse = 1.0 / counts[0].astype(jnp.float32)
    sent, sums = code(grads, momentum, inverse)
    owned = exchange(sent)
    grads, momentum, _ = lax.optimization_barrier((grads, momentum, sent))
    velocity = momentum_rate * momentum.astype(jnp.float32) + grads * inverse
    update = exchange(orthogonalize(owned, sum_over_devices(sums))).astype(jnp.float32)
    emb_new = adamw(emb_grad, emb_weight, emb_first, emb_second, inverse)
    gain_new = adamw(gain_grad, gain_weight, gain_first, gain_second, inverse)
    return (
        velocity.astype(jnp.bfloat16),
        update,
        emb_new[0],
        emb_new[1],
        emb_new[2],
        gain_new[0],
        gain_new[1],
        gain_new[2],
    )


def solution(mesh):
    placed = (
        P(None, "shard", "tensor"),
        P(None, "shard", "tensor"),
        P(),
        P("shard", "tensor"),
        P("shard", "tensor"),
        P("shard", "tensor"),
        P("shard", "tensor"),
        P(("shard", "tensor")),
        P(("shard", "tensor")),
        P(("shard", "tensor")),
        P(("shard", "tensor")),
    )
    return jax.shard_map(
        body,
        mesh=mesh,
        in_specs=placed,
        out_specs=(
            P(None, "shard", "tensor"),
            P(None, "shard", "tensor"),
            P("shard", "tensor"),
            P("shard", "tensor"),
            P("shard", "tensor"),
            P(("shard", "tensor")),
            P(("shard", "tensor")),
            P(("shard", "tensor")),
        ),
        check_vma=False,
    )
```

```python
import functools
import math

import jax
import jax.numpy as jnp
from jax import lax
from jax.experimental import pallas as pl
from jax.experimental.pallas import tpu as pltpu
from jax.sharding import PartitionSpec as P

D = 2048
NS_STEPS = 4
CORES = 2
EDGE = 256
LIFT = 2.0**25
PARTS = 4
PACE = 2

linear_coef = 3.4445
cubic_coef = -4.775
quintic_coef = 2.0315
momentum_rate = 0.95
learn_rate = 0.01
decay_weight = 0.1
first_rate = 0.9
second_rate = 0.95
adam_floor = 1e-08
norm_floor = 1e-07


def adamw(grad, weight, first, second, inverse):
    scaled = grad * inverse
    first_new = first_rate * first + (1.0 - first_rate) * scaled
    second_new = second_rate * second + (1.0 - second_rate) * scaled * scaled
    weight_new = weight - learn_rate * (
        first_new / (jnp.sqrt(second_new) + adam_floor) + decay_weight * weight
    )
    return (weight_new, first_new, second_new)


def span(index):
    return slice(index * EDGE, (index + 1) * EDGE)


def upper_blocks(width):
    return [(i, j) for j in range(width // EDGE) for i in range(j + 1)]


def write_gram(turned_ref, gram_ref):
    for j in reversed(range(turned_ref.shape[0] // EDGE)):
        part = lax.dot_general(
            turned_ref[: (j + 1) * EDGE, :],
            turned_ref[span(j), :],
            (((1,), (1,)), ((), ())),
            preferred_element_type=jnp.float32,
        )
        for i in range(j + 1):
            gram_ref[j * (j + 1) // 2 + i] = part[span(i), :].astype(jnp.bfloat16)


def symmetric(left, right, finish, out):
    for j in reversed(range(out.shape[0] // EDGE)):
        product = jnp.dot(
            left[: (j + 1) * EDGE, :], right[:, span(j)], preferred_element_type=jnp.float32
        )
        for i in range(j + 1):
            place = (span(i), span(j))
            block = finish(place, product[span(i), :]).astype(jnp.bfloat16)
            out[place] = block
            if i != j:
                out[span(j), span(i)] = block.T


def write_factor(own_ref, other_ref, gram, poly, spare, later):
    def read(ref, place):
        return ref[place].astype(jnp.float32)

    def polynomial(grams, out):
        symmetric(
            grams,
            grams,
            lambda place, square: cubic_coef * read(grams, place) + quintic_coef * square,
            out,
        )

    for slot, (i, j) in enumerate(upper_blocks(gram.shape[0])):
        block = own_ref[slot].astype(jnp.float32) + other_ref[slot].astype(jnp.float32)
        block = block.astype(jnp.bfloat16)
        gram[span(i), span(j)] = block
        if i != j:
            gram[span(j), span(i)] = block.T
    polynomial(gram, poly)
    symmetric(
        poly, poly, lambda place, square: 2.0 * linear_coef * read(poly, place) + square, spare
    )
    symmetric(
        gram, spare, lambda place, change: linear_coef**2 * read(gram, place) + change, later
    )
    polynomial(later, gram)
    symmetric(
        poly,
        gram,
        lambda place, both: linear_coef * (read(poly, place) + read(gram, place)) + both,
        spare,
    )


def send_kernel(
    inverse_ref, grads_ref, momentum_ref, sent_ref, sums_ref, grads, momentum, sems
):
    grad_part = LIFT * (1.0 + momentum_rate) * inverse_ref[0]
    momentum_part = LIFT * momentum_rate**2
    matrices, rows, cols = grads.shape
    parts = matrices // PACE
    arrivals = []
    for p in range(parts):
        part = pl.ds(p * PACE, PACE)
        arrivals.append(
            [
                pltpu.make_async_copy(grads_ref.at[part], grads.at[part], sems.at[2 * p]),
                pltpu.make_async_copy(momentum_ref.at[part], momentum.at[part], sems.at[2 * p + 1]),
            ]
        )
        for copy in arrivals[-1]:
            copy.start()
    for p in range(parts):
        for copy in arrivals[p]:
            copy.wait()
        for k in range(p * PACE, (p + 1) * PACE):
            lifted = grad_part * grads[k] + momentum_part * momentum[k].astype(jnp.float32)
            squares = lifted * lifted
            sent_ref[k] = (squares * (lifted * jnp.abs(lifted))).astype(jnp.bfloat16)
            squares = squares.reshape(rows // 8, 8, cols).sum(axis=0)
            sums_ref[k] = sum(squares[:, c : c + 128] for c in range(0, cols, 128))


def first_kernel(totals_ref, chip_ref, block_ref, turned_ref, gram_ref, *, tensor):
    scale = 1.0 / (jnp.sqrt(jnp.full((1, 1), totals_ref[chip_ref[0]], jnp.float32)) + LIFT * norm_floor)
    blocks, rows, cols = block_ref.shape
    for s in range(blocks // tensor):
        for t in range(tensor):
            power = block_ref[s * tensor + t].T.astype(jnp.float32)
            root = lax.rsqrt(lax.rsqrt(jnp.abs(power))) * scale
            iterate = jnp.where(power < 0.0, -root, root).astype(jnp.bfloat16)
            turned_ref[t * cols : (t + 1) * cols, s * rows : (s + 1) * rows] = iterate
    write_gram(turned_ref, gram_ref)


def middle_kernel(turned_ref, own_ref, other_ref, next_ref, gram_ref, *squares):
    write_factor(own_ref, other_ref, *squares)
    factor = squares[2]
    for c in range(turned_ref.shape[0] // EDGE):
        new = linear_coef**2 * turned_ref[span(c), :].astype(jnp.float32) + jnp.dot(
            factor[span(c), :], turned_ref[...], preferred_element_type=jnp.float32
        )
        next_ref[span(c), :] = new.astype(jnp.bfloat16)
    write_gram(next_ref, gram_ref)


def flip_kernel(turned_ref, straight_ref):
    for c in range(turned_ref.shape[1] // EDGE):
        straight_ref[span(c), :] = turned_ref[:, span(c)].T


def last_kernel(straight_ref, own_ref, other_ref, block_ref, finished, sems, *squares, tensor):
    write_factor(own_ref, other_ref, *squares)
    factor = squares[2]
    blocks, rows, cols = block_ref.shape
    height = straight_ref.shape[0]
    copies = []
    for p in range(PARTS):
        top, bottom = p * height // PARTS, (p + 1) * height // PARTS
        old = straight_ref[top:bottom, :]
        new = linear_coef**2 * old.astype(jnp.float32) + jnp.dot(
            old, factor[...], preferred_element_type=jnp.float32
        )
        new = (math.sqrt(D) * new).astype(jnp.bfloat16)
        for s in range(top // rows, bottom // rows):
            for t in range(tensor):
                finished[s * tensor + t] = new[
                    s * rows - top : (s + 1) * rows - top, t * cols : (t + 1) * cols
                ]
        part = pl.ds(p * (blocks // PARTS), blocks // PARTS)
        copies.append(
            pltpu.make_async_copy(finished.at[part], block_ref.at[part], sems.at[p])
        )
        copies[-1].start()
    for copy in copies:
        copy.wait()


limits = pltpu.CompilerParams(vmem_limit_bytes=20 * 2**20)
streamed = pltpu.CompilerParams(vmem_limit_bytes=60 * 2**20)


def run_kernel(kernel, results, scratch, *operands, out=pltpu.VMEM):
    whole = pl.BlockSpec(memory_space=pltpu.VMEM)
    scalar = pl.BlockSpec(memory_space=pltpu.SMEM)
    return pl.pallas_call(
        kernel,
        out_shape=results,
        in_specs=[scalar if value.ndim == 1 else whole for value in operands],
        out_specs=[pl.BlockSpec(memory_space=out)] * len(results),
        scratch_shapes=scratch,
        compiler_params=limits,
    )(*operands)


def code(grads, momentum, inverse):
    whole = pl.BlockSpec(memory_space=pl.ANY)
    sent, sums = pl.pallas_call(
        send_kernel,
        out_shape=[
            jax.ShapeDtypeStruct(grads.shape, jnp.bfloat16),
            jax.ShapeDtypeStruct((grads.shape[0], 8, 128), jnp.float32),
        ],
        in_specs=[pl.BlockSpec(memory_space=pltpu.SMEM), whole, whole],
        out_specs=[pl.BlockSpec(memory_space=pltpu.VMEM)] * 2,
        scratch_shapes=[
            pltpu.VMEM(grads.shape, jnp.float32),
            pltpu.VMEM(grads.shape, jnp.bfloat16),
            pltpu.SemaphoreType.DMA((2 * grads.shape[0] // PACE,)),
        ],
        compiler_params=streamed,
    )(inverse.reshape(1), grads, momentum)
    return sent, jnp.sum(sums, axis=(1, 2))


def other_core(value):
    shards = lax.axis_size("shard")
    return lax.ppermute(value, "shard", [(i, i ^ 1) for i in range(shards)])


def chip_groups():
    shards, tensor = lax.axis_size("shard"), lax.axis_size("tensor")
    return [
        [s * tensor + t for s in range(core, shards, CORES) for t in range(tensor)]
        for core in range(CORES)
    ]


def exchange(blocks):
    return lax.all_to_all(
        blocks,
        ("shard", "tensor"),
        split_axis=0,
        concat_axis=0,
        axis_index_groups=chip_groups(),
        tiled=True,
    )


def orthogonalize(blocks, totals):
    tensor = lax.axis_size("tensor")
    chip = (lax.axis_index("shard") // CORES * tensor + lax.axis_index("tensor")).reshape(1)
    width = tensor * blocks.shape[2]
    height = blocks.shape[0] // tensor * blocks.shape[1]
    turned_type = jax.ShapeDtypeStruct((width, height), jnp.bfloat16)
    gram_type = jax.ShapeDtypeStruct((len(upper_blocks(width)), EDGE, EDGE), jnp.bfloat16)
    squares = [pltpu.VMEM((width, width), jnp.bfloat16)] * 4
    turned, own = run_kernel(
        functools.partial(first_kernel, tensor=tensor), [turned_type, gram_type], [], totals, chip, blocks
    )
    for _ in range(NS_STEPS // 2 - 1):
        turned, own = run_kernel(
            middle_kernel, [turned_type, gram_type], squares, turned, own, other_core(own)
        )
    straight_type = jax.ShapeDtypeStruct((height, width), jnp.bfloat16)
    straight = run_kernel(flip_kernel, [straight_type], [], turned)[0]
    return run_kernel(
        functools.partial(last_kernel, tensor=tensor),
        [jax.ShapeDtypeStruct(blocks.shape, jnp.bfloat16)],
        [pltpu.VMEM(blocks.shape, jnp.bfloat16), pltpu.SemaphoreType.DMA((PARTS,))] + squares,
        straight,
        own,
        other_core(own),
        out=pl.ANY,
    )[0]


def sum_over_devices(values):
    devices = lax.axis_size("shard") * lax.axis_size("tensor")
    bits = [1 << k for k in range(devices.bit_length() - 1)]
    bits[-1] += bits[-2]
    for bit in bits:
        pairs = [(i, i ^ bit) for i in range(devices)]
        values = values + lax.ppermute(values, ("shard", "tensor"), pairs)
    return values


def body(
    grads,
    momentum,
    counts,
    emb_grad,
    emb_weight,
    emb_first,
    emb_second,
    gain_grad,
    gain_weight,
    gain_first,
    gain_second,
):
    inverse = 1.0 / counts[0].astype(jnp.float32)
    sent, sums = code(grads, momentum, inverse)
    owned = exchange(sent)
    grads, momentum, _ = lax.optimization_barrier((grads, momentum, sent))
    velocity = momentum_rate * momentum.astype(jnp.float32) + grads * inverse
    update = exchange(orthogonalize(owned, sum_over_devices(sums))).astype(jnp.float32)
    emb_new = adamw(emb_grad, emb_weight, emb_first, emb_second, inverse)
    gain_new = adamw(gain_grad, gain_weight, gain_first, gain_second, inverse)
    return (
        velocity.astype(jnp.bfloat16),
        update,
        emb_new[0],
        emb_new[1],
        emb_new[2],
        gain_new[0],
        gain_new[1],
        gain_new[2],
    )


def solution(mesh):
    placed = (
        P(None, "shard", "tensor"),
        P(None, "shard", "tensor"),
        P(),
        P("shard", "tensor"),
        P("shard", "tensor"),
        P("shard", "tensor"),
        P("shard", "tensor"),
        P(("shard", "tensor")),
        P(("shard", "tensor")),
        P(("shard", "tensor")),
        P(("shard", "tensor")),
    )
    return jax.shard_map(
        body,
        mesh=mesh,
        in_specs=placed,
        out_specs=(
            P(None, "shard", "tensor"),
            P(None, "shard", "tensor"),
            P("shard", "tensor"),
            P("shard", "tensor"),
            P("shard", "tensor"),
            P(("shard", "tensor")),
            P(("shard", "tensor")),
            P(("shard", "tensor")),
        ),
        check_vma=False,
    )
```

```python
import functools
import math

import jax
import jax.numpy as jnp
from jax import lax
from jax.experimental import pallas as pl
from jax.experimental.pallas import tpu as pltpu
from jax.sharding import PartitionSpec as P

D = 2048
NS_STEPS = 4
CORES = 2
EDGE = 256
LIFT = 2.0**25
PARTS = 4
PACE = 2

linear_coef = 3.4445
cubic_coef = -4.775
quintic_coef = 2.0315
momentum_rate = 0.95
learn_rate = 0.01
decay_weight = 0.1
first_rate = 0.9
second_rate = 0.95
adam_floor = 1e-08
norm_floor = 1e-07


def adamw(grad, weight, first, second, inverse):
    scaled = grad * inverse
    first_new = first_rate * first + (1.0 - first_rate) * scaled
    second_new = second_rate * second + (1.0 - second_rate) * scaled * scaled
    weight_new = weight - learn_rate * (
        first_new / (jnp.sqrt(second_new) + adam_floor) + decay_weight * weight
    )
    return (weight_new, first_new, second_new)


def span(index):
    return slice(index * EDGE, (index + 1) * EDGE)


def upper_blocks(width):
    return [(i, j) for j in range(width // EDGE) for i in range(j + 1)]


def write_gram(turned_ref, gram_ref):
    for j in reversed(range(turned_ref.shape[0] // EDGE)):
        part = lax.dot_general(
            turned_ref[: (j + 1) * EDGE, :],
            turned_ref[span(j), :],
            (((1,), (1,)), ((), ())),
            preferred_element_type=jnp.float32,
        )
        for i in range(j + 1):
            gram_ref[j * (j + 1) // 2 + i] = part[span(i), :].astype(jnp.bfloat16)


def symmetric(left, right, finish, out):
    for j in reversed(range(out.shape[0] // EDGE)):
        product = jnp.dot(
            left[: (j + 1) * EDGE, :], right[:, span(j)], preferred_element_type=jnp.float32
        )
        for i in range(j + 1):
            place = (span(i), span(j))
            block = finish(place, product[span(i), :]).astype(jnp.bfloat16)
            out[place] = block
            if i != j:
                out[span(j), span(i)] = block.T


def write_factor(own_ref, other_ref, gram, poly, spare, later):
    def read(ref, place):
        return ref[place].astype(jnp.float32)

    def polynomial(grams, out):
        symmetric(
            grams,
            grams,
            lambda place, square: cubic_coef * read(grams, place) + quintic_coef * square,
            out,
        )

    for slot, (i, j) in enumerate(upper_blocks(gram.shape[0])):
        block = own_ref[slot].astype(jnp.float32) + other_ref[slot].astype(jnp.float32)
        block = block.astype(jnp.bfloat16)
        gram[span(i), span(j)] = block
        if i != j:
            gram[span(j), span(i)] = block.T
    polynomial(gram, poly)
    symmetric(
        poly, poly, lambda place, square: 2.0 * linear_coef * read(poly, place) + square, spare
    )
    symmetric(
        gram, spare, lambda place, change: linear_coef**2 * read(gram, place) + change, later
    )
    polynomial(later, gram)
    symmetric(
        poly,
        gram,
        lambda place, both: linear_coef * (read(poly, place) + read(gram, place)) + both,
        spare,
    )


def send_kernel(
    inverse_ref, grads_ref, momentum_ref, sent_ref, sums_ref, grads, momentum, sems
):
    grad_part = LIFT * (1.0 + momentum_rate) * inverse_ref[0]
    momentum_part = LIFT * momentum_rate**2
    matrices, rows, cols = grads.shape
    parts = matrices // PACE
    arrivals = []
    for p in range(parts):
        part = pl.ds(p * PACE, PACE)
        arrivals.append(
            [
                pltpu.make_async_copy(grads_ref.at[part], grads.at[part], sems.at[2 * p]),
                pltpu.make_async_copy(momentum_ref.at[part], momentum.at[part], sems.at[2 * p + 1]),
            ]
        )
        for copy in arrivals[-1]:
            copy.start()
    for p in range(parts):
        for copy in arrivals[p]:
            copy.wait()
        for k in range(p * PACE, (p + 1) * PACE):
            lifted = grad_part * grads[k] + momentum_part * momentum[k].astype(jnp.float32)
            squares = lifted * lifted
            sent_ref[k] = (squares * (lifted * jnp.abs(lifted))).astype(jnp.bfloat16)
            squares = squares.reshape(rows // 8, 8, cols).sum(axis=0)
            sums_ref[k] = sum(squares[:, c : c + 128] for c in range(0, cols, 128))


def first_kernel(totals_ref, chip_ref, block_ref, turned_ref, gram_ref, *, tensor):
    scale = 1.0 / (jnp.sqrt(jnp.full((1, 1), totals_ref[chip_ref[0]], jnp.float32)) + LIFT * norm_floor)
    blocks, rows, cols = block_ref.shape
    for s in range(blocks // tensor):
        for t in range(tensor):
            power = block_ref[s * tensor + t].T.astype(jnp.float32)
            root = lax.rsqrt(lax.rsqrt(jnp.abs(power))) * scale
            iterate = jnp.where(power < 0.0, -root, root).astype(jnp.bfloat16)
            turned_ref[t * cols : (t + 1) * cols, s * rows : (s + 1) * rows] = iterate
    write_gram(turned_ref, gram_ref)


def middle_kernel(turned_ref, own_ref, other_ref, next_ref, gram_ref, *squares):
    write_factor(own_ref, other_ref, *squares)
    factor = squares[2]
    for c in range(turned_ref.shape[0] // EDGE):
        new = linear_coef**2 * turned_ref[span(c), :].astype(jnp.float32) + jnp.dot(
            factor[span(c), :], turned_ref[...], preferred_element_type=jnp.float32
        )
        next_ref[span(c), :] = new.astype(jnp.bfloat16)
    write_gram(next_ref, gram_ref)


def flip_kernel(turned_ref, straight_ref):
    for c in range(turned_ref.shape[1] // EDGE):
        straight_ref[span(c), :] = turned_ref[:, span(c)].T


def last_kernel(straight_ref, own_ref, other_ref, block_ref, finished, sems, *squares, tensor):
    write_factor(own_ref, other_ref, *squares)
    factor = squares[2]
    blocks, rows, cols = block_ref.shape
    groups = blocks // tensor
    copies = []
    for s in range(groups):
        old = straight_ref[s * rows : (s + 1) * rows, :]
        new = linear_coef**2 * old.astype(jnp.float32) + jnp.dot(
            old, factor[...], preferred_element_type=jnp.float32
        )
        new = (math.sqrt(D) * new).astype(jnp.bfloat16)
        for t in range(tensor):
            finished[s * tensor + t] = new[:, t * cols : (t + 1) * cols]
        if (s + 1) % (groups // PARTS) == 0:
            part = pl.ds(len(copies) * (blocks // PARTS), blocks // PARTS)
            copies.append(
                pltpu.make_async_copy(
                    finished.at[part], block_ref.at[part], sems.at[len(copies)]
                )
            )
            copies[-1].start()
    for copy in copies:
        copy.wait()


limits = pltpu.CompilerParams(vmem_limit_bytes=20 * 2**20)
streamed = pltpu.CompilerParams(vmem_limit_bytes=60 * 2**20)


def run_kernel(kernel, results, scratch, *operands, out=pltpu.VMEM):
    whole = pl.BlockSpec(memory_space=pltpu.VMEM)
    scalar = pl.BlockSpec(memory_space=pltpu.SMEM)
    return pl.pallas_call(
        kernel,
        out_shape=results,
        in_specs=[scalar if value.ndim == 1 else whole for value in operands],
        out_specs=[pl.BlockSpec(memory_space=out)] * len(results),
        scratch_shapes=scratch,
        compiler_params=limits,
    )(*operands)


def code(grads, momentum, inverse):
    whole = pl.BlockSpec(memory_space=pl.ANY)
    sent, sums = pl.pallas_call(
        send_kernel,
        out_shape=[
            jax.ShapeDtypeStruct(grads.shape, jnp.bfloat16),
            jax.ShapeDtypeStruct((grads.shape[0], 8, 128), jnp.float32),
        ],
        in_specs=[pl.BlockSpec(memory_space=pltpu.SMEM), whole, whole],
        out_specs=[pl.BlockSpec(memory_space=pltpu.VMEM)] * 2,
        scratch_shapes=[
            pltpu.VMEM(grads.shape, jnp.float32),
            pltpu.VMEM(grads.shape, jnp.bfloat16),
            pltpu.SemaphoreType.DMA((2 * grads.shape[0] // PACE,)),
        ],
        compiler_params=streamed,
    )(inverse.reshape(1), grads, momentum)
    return sent, jnp.sum(sums, axis=(1, 2))


def other_core(value):
    shards = lax.axis_size("shard")
    return lax.ppermute(value, "shard", [(i, i ^ 1) for i in range(shards)])


def chip_groups():
    shards, tensor = lax.axis_size("shard"), lax.axis_size("tensor")
    return [
        [s * tensor + t for s in range(core, shards, CORES) for t in range(tensor)]
        for core in range(CORES)
    ]


def exchange(blocks):
    return lax.all_to_all(
        blocks,
        ("shard", "tensor"),
        split_axis=0,
        concat_axis=0,
        axis_index_groups=chip_groups(),
        tiled=True,
    )


def orthogonalize(blocks, totals):
    tensor = lax.axis_size("tensor")
    chip = (lax.axis_index("shard") // CORES * tensor + lax.axis_index("tensor")).reshape(1)
    width = tensor * blocks.shape[2]
    height = blocks.shape[0] // tensor * blocks.shape[1]
    turned_type = jax.ShapeDtypeStruct((width, height), jnp.bfloat16)
    gram_type = jax.ShapeDtypeStruct((len(upper_blocks(width)), EDGE, EDGE), jnp.bfloat16)
    squares = [pltpu.VMEM((width, width), jnp.bfloat16)] * 4
    turned, own = run_kernel(
        functools.partial(first_kernel, tensor=tensor), [turned_type, gram_type], [], totals, chip, blocks
    )
    for _ in range(NS_STEPS // 2 - 1):
        turned, own = run_kernel(
            middle_kernel, [turned_type, gram_type], squares, turned, own, other_core(own)
        )
    straight_type = jax.ShapeDtypeStruct((height, width), jnp.bfloat16)
    straight = run_kernel(flip_kernel, [straight_type], [], turned)[0]
    return run_kernel(
        functools.partial(last_kernel, tensor=tensor),
        [jax.ShapeDtypeStruct(blocks.shape, jnp.bfloat16)],
        [pltpu.VMEM(blocks.shape, jnp.bfloat16), pltpu.SemaphoreType.DMA((PARTS,))] + squares,
        straight,
        own,
        other_core(own),
        out=pl.ANY,
    )[0]


def sum_over_devices(values):
    devices = lax.axis_size("shard") * lax.axis_size("tensor")
    bits = [1 << k for k in range(devices.bit_length() - 1)]
    bits[-1] += bits[-2]
    for bit in bits:
        pairs = [(i, i ^ bit) for i in range(devices)]
        values = values + lax.ppermute(values, ("shard", "tensor"), pairs)
    return values


def body(
    grads,
    momentum,
    counts,
    emb_grad,
    emb_weight,
    emb_first,
    emb_second,
    gain_grad,
    gain_weight,
    gain_first,
    gain_second,
):
    inverse = 1.0 / counts[0].astype(jnp.float32)
    sent, sums = code(grads, momentum, inverse)
    owned = exchange(sent)
    grads, momentum, _ = lax.optimization_barrier((grads, momentum, sent))
    velocity = momentum_rate * momentum.astype(jnp.float32) + grads * inverse
    emb_new = adamw(emb_grad, emb_weight, emb_first, emb_second, inverse)
    momentum_new = velocity.astype(jnp.bfloat16)
    owned, momentum_new, emb_new = lax.optimization_barrier((owned, momentum_new, emb_new))
    update = exchange(orthogonalize(owned, sum_over_devices(sums))).astype(jnp.float32)
    gain_new = adamw(gain_grad, gain_weight, gain_first, gain_second, inverse)
    return (
        momentum_new,
        update,
        emb_new[0],
        emb_new[1],
        emb_new[2],
        gain_new[0],
        gain_new[1],
        gain_new[2],
    )


def solution(mesh):
    placed = (
        P(None, "shard", "tensor"),
        P(None, "shard", "tensor"),
        P(),
        P("shard", "tensor"),
        P("shard", "tensor"),
        P("shard", "tensor"),
        P("shard", "tensor"),
        P(("shard", "tensor")),
        P(("shard", "tensor")),
        P(("shard", "tensor")),
        P(("shard", "tensor")),
    )
    return jax.shard_map(
        body,
        mesh=mesh,
        in_specs=placed,
        out_specs=(
            P(None, "shard", "tensor"),
            P(None, "shard", "tensor"),
            P("shard", "tensor"),
            P("shard", "tensor"),
            P("shard", "tensor"),
            P(("shard", "tensor")),
            P(("shard", "tensor")),
            P(("shard", "tensor")),
        ),
        check_vma=False,
    )
```
